512 devices in a mesh: occ: 8 (over x, core), vir: 64 (over z, y).
Axes of the slice: x: 4, y: 4, z: 16, core: 2. Of those that a mesh axis runs over, the one named last changes fastest.
Arguments:
- amplitudes: bfloat16 [3072, 128, 128], P('occ', 'vir'), may hold values from -6 to 6
- amp_blocks: int32 [128], P('vir'), may hold values from 0 to 255, as said below
- integrals: bfloat16 [64, 128, 128, 128], P('vir', 'occ'), may hold values from -0.125 to 0.125
- integral_rows: int32 [64, 128], P('vir', 'occ'), may hold values from -1 to 255, as said below
- integral_cols: int32 [64, 128], P('vir', 'occ'), may hold values from 0 to 255, as said below
Outputs:
- ladder: bfloat16 [3072, 256, 128], P('occ', 'vir')
The draws below stay inside these ranges and needn't reach their ends.
Inputs may be any that keep to these rules, and one draw needn't show every extreme that they name: `amp_blocks`: distinct pair blocks. `integral_rows`: each entry is -1 (empty slot) or one of amp_blocks; live pairs (row, column) of one owner are distinct; one owner's live slots name each amplitude block at most once; every owner's slots have some live ones, and some owner has all 128 live. `integral_cols`: row v holds blocks v * 4 to v * 4 + 3.
All inputs are finite; a program needn't handle non-finite values.
Results may differ from the reference program's by a relative error of at most 0.0013.
Values may be sent and summed in bfloat16 or wider, within the bound.
A program may use at most 128 MiB of HBM per device.

```python
import jax
import jax.numpy as jnp
from jax import lax

TILE = 128
OBLK = 4
ISLOT = 128
ABLK = 128
NBLK = 256
OCC_ROWS = 3072
N_OCC = 8
N_VIR = 64


def shared_layout(key):
    ids = jax.random.permutation(key, NBLK)[:ABLK].astype(jnp.int32)
    perm_keys = jax.random.split(jax.random.fold_in(key, 11), N_VIR)
    perms = jax.vmap(lambda one: jax.random.permutation(one, ABLK))(perm_keys).astype(jnp.int32)
    slot = jnp.arange(ISLOT).astype(jnp.int32)
    pick = perms[:, slot % ABLK]
    rows = ids[pick]
    shift = jax.random.randint(jax.random.fold_in(key, 12), (N_VIR, ABLK), 0, OBLK).astype(jnp.int32)
    local_col = (slot[None, :] // ABLK + jnp.take_along_axis(shift, pick, axis=1)) % OBLK
    cols = jnp.arange(N_VIR).astype(jnp.int32)[:, None] * OBLK + local_col
    width = ISLOT // N_OCC
    counts = jax.random.randint(jax.random.fold_in(key, 13), (N_VIR, N_OCC), width // 4, width + 1).astype(jnp.int32)
    busy = jax.random.randint(jax.random.fold_in(key, 14), (), 0, N_VIR).astype(jnp.int32)
    counts = jnp.where(jnp.arange(N_VIR).astype(jnp.int32)[:, None] == busy, width, counts)
    shard = slot // width
    position = slot % width
    live = position[None, :] < counts[:, shard]
    rows = jnp.where(live, rows, -1)
    return (ids, rows.astype(jnp.int32), cols.astype(jnp.int32))


def draw_amp_blocks(key, part):
    ids, rows, cols = shared_layout(key)
    return ids


def draw_integral_rows(key, part):
    ids, rows, cols = shared_layout(key)
    return rows


def draw_integral_cols(key, part):
    ids, rows, cols = shared_layout(key)
    return cols


def level_of(rng, shape, pieces, low, top_value):
    def one(dim, shards_of):
        steps = jax.random.uniform(jax.random.fold_in(jax.random.fold_in(rng, 6), dim), (shards_of,), jnp.float32, low / len(pieces), top_value / len(pieces))
        return jnp.repeat(jnp.exp(steps), shape[dim] // shards_of).reshape((-1,) + (1,) * (len(shape) - dim - 1))

    factor_of = one(*pieces[0])
    for cut in pieces[1:]:
        factor_of = factor_of * one(*cut)
    return factor_of


def centred(own_key, dims, spread, reach, cuts=(), held_as=jnp.bfloat16):
    level = level_of(own_key, dims, cuts, -0.22, 0.18) if cuts else 1.0
    array = jax.random.normal(own_key, dims, jnp.float32) * spread * level
    return jnp.minimum(jnp.maximum(array, -reach), reach).astype(held_as)


def setup_inputs(seed: int = 0) -> dict:
    key_list = jax.random.split(jax.random.key(seed), 6)
    amplitudes = centred(key_list[0], (OCC_ROWS, ABLK, TILE), 1.0, 6.0, ((0, 8), (1, 64)))
    amp_blocks = draw_amp_blocks(jax.random.fold_in(key_list[5], 71), 0)
    integrals = centred(key_list[2], (N_VIR, ISLOT, TILE, TILE), (TILE * 16) ** -0.5, 0.125, ((0, 64), (1, 8)))
    integral_rows = draw_integral_rows(jax.random.fold_in(key_list[5], 71), 0)
    integral_cols = draw_integral_cols(jax.random.fold_in(key_list[5], 71), 0)
    return dict(amplitudes=amplitudes, amp_blocks=amp_blocks, integrals=integrals, integral_rows=integral_rows, integral_cols=integral_cols)


def reference(amplitudes, amp_blocks, integrals, integral_rows, integral_cols):
    known = jnp.arange(ABLK).astype(jnp.int32)
    match = integral_rows[:, :, None] == amp_blocks[None, None, :]
    slots = jnp.sum(jnp.where(match, known[None, None, :], 0), axis=2).astype(jnp.int32)
    live = integral_rows >= 0
    owners = jnp.arange(N_VIR).astype(jnp.int32)
    columns = jnp.arange(OBLK).astype(jnp.int32)

    def per_owner(carry, packed):
        tiles, slot_row, live_row, col_row, owner = packed
        picked = jnp.take(amplitudes, slot_row, axis=1).astype(jnp.float32)
        prod = jnp.einsum("rkt,ktu->rku", picked, tiles.astype(jnp.float32))
        onehot = ((col_row - owner * OBLK)[:, None] == columns[None, :]) & live_row[:, None]
        return carry, jnp.einsum("rku,kc->rcu", prod, onehot.astype(prod.dtype), precision=lax.Precision.HIGHEST)

    unused, blocks = lax.scan(per_owner, jnp.zeros((), jnp.float32), (integrals, slots, live, integral_cols, owners))
    ladder = jnp.transpose(blocks, (1, 0, 2, 3)).reshape(OCC_ROWS, NBLK, TILE)
    return ladder.astype(jnp.bfloat16)
```

```python
import functools

import jax
import jax.numpy as jnp
from jax import lax
from jax.experimental import pallas as pl
from jax.experimental.pallas import tpu as pltpu
from jax.sharding import PartitionSpec as P

MESH = pl.DeviceIdType.MESH
OBLK = 4
TILE = 128
NX, NY, NZ = 4, 4, 16
SUB = 96
CHUNK = 8
NS = 128
GROUPS = ((0, 0), (0, 1), (0, 3), (1, 0), (0, 2), (1, 1), (1, 3), (1, 2))


def kernel(
    a_in, w_in, blocks, rows, cols, out_ref,
    a_src, a_all, id_all, w_all, wi_all, acc, wide, stage, id_own, wi_own, merged, info, table,
    a0_send, a0_recv, z_send, z_recv, zi_send, zi_recv, d_send, d_recv,
    own_send, owni_send, w_recv, wi_recv, f_send, fi_send, out_send, out_recv, info_sem,
):
    occ, vir = lax.axis_index("occ"), lax.axis_index("vir")
    x, c = occ // 2, lax.rem(occ, 2)
    z, y = vir // NY, lax.rem(vir, NY)
    home = y // 2
    unmatched = (c + home) % 2
    oy = lax.rem(y, 2)

    def dev(xx, cc, yy, zz):
        return (lax.rem(xx + NX, NX) * 2 + cc, lax.rem(zz + NZ, NZ) * NY + lax.rem(yy + NY, NY))

    def remote(src, dst, send, recv, device):
        return pltpu.make_async_remote_copy(
            src_ref=src, dst_ref=dst, send_sem=send, recv_sem=recv, device_id=device, device_id_type=MESH
        )

    def landed(ref, sem):
        pltpu.make_async_copy(ref, ref, sem).wait()

    partners = [dev(x, (c + k) % 2, y + j, z) for j in range(NY) for k in range(2) if (j, k) != (0, 0)]
    partners += [dev(x + s, k, y, z) for s in (1, -1) for k in range(2)]
    partners += [dev(x, c, y, z + s) for s in (1, -1)]
    barrier = pltpu.get_barrier_semaphore()
    for p in partners:
        pl.semaphore_signal(barrier, inc=1, device_id=p, device_id_type=MESH)

    wide[...] = a_in[...].astype(jnp.float32)
    for b in range(2):
        a_src[b] = wide[pl.ds(b, NY * SUB, stride=2), :].astype(jnp.bfloat16)
    sub = lax.broadcasted_iota(jnp.int32, (8, TILE), 0)
    lane = lax.broadcasted_iota(jnp.int32, (8, TILE), 1)
    place_of = sub * TILE + lane
    mark = jnp.zeros((8, TILE), jnp.int32)
    for b in range(2):
        mark = jnp.where(place_of == blocks[b], 2 * vir + b, mark)
    id_own[...] = mark
    mark = jnp.zeros((8, TILE), jnp.int32)
    for t in range(2 * CHUNK):
        here = lane == occ * 2 * CHUNK + t
        mark = jnp.where(here & (sub == 2), rows[0, t], mark)
        local = jnp.where(rows[0, t] >= 0, cols[0, t] - vir * OBLK, OBLK)
        mark = jnp.where(here & (sub == 3), local, mark)
    wi_own[...] = mark
    acc[...] = jnp.zeros_like(acc)

    pl.semaphore_wait(barrier, len(partners))

    a_local = []
    for b in range(2):
        a_local.append(pltpu.make_async_copy(a_src.at[b, pl.ds(y * SUB, SUB)], a_all.at[c, 2 * vir + b], a0_recv.at[0, b]))
    a_local.append(pltpu.make_async_copy(id_own, id_all.at[vir], a0_recv.at[0, 2]))
    for copy in a_local:
        copy.start()
    a0 = []
    for k in (1, 3, 2):
        to = lax.rem(y + k, NY)
        for b in range(2):
            src = a_src.at[b, pl.ds(to * SUB, SUB)]
            a0.append(remote(src, a_all.at[c, 2 * vir + b], a0_send.at[k, b], a0_recv.at[k, b], dev(x, c, to, z)))
        a0.append(remote(id_own, id_all.at[vir], a0_send.at[k, 2], a0_recv.at[k, 2], dev(x, c, to, z)))
    for copy in a0:
        copy.start()

    mine, mine_sem = w_all.at[oy, x, c], w_recv.at[oy, x, c]
    targets = (dev(x + 1, home, y, z), dev(x - 1, home, y, z), dev(x, home, y + 1, z), dev(x, home, y - 1, z))
    beside = dev(x, home, y, z)
    w_src = [w_in.at[0, pl.ds(r * CHUNK, CHUNK)] for r in range(2)]

    def own_tiles(r, d, to):
        return remote(w_src[r], mine.at[r], own_send.at[r, d], mine_sem.at[r], to)

    def own_marks(d, to):
        return remote(wi_own, wi_all.at[oy, x, c], owni_send.at[d], wi_recv.at[oy, x, c], to)

    def own_start(ds):
        for r in range(2):
            for d in ds:
                own_tiles(r, d, targets[d]).start()
                if r == 0:
                    own_marks(d, targets[d]).start()

    def own_beside():
        @pl.when(unmatched == 0)
        def _():
            for r in range(2):
                pltpu.make_async_copy(w_src[r], mine.at[r], mine_sem.at[r]).start()
            pltpu.make_async_copy(wi_own, wi_all.at[oy, x, c], wi_recv.at[oy, x, c]).start()

        @pl.when(unmatched == 1)
        def _():
            for r in range(2):
                own_tiles(r, 4, beside).start()
            own_marks(4, beside).start()

    def zchunk(ref, zz, lo, n, per):
        return ref.at[pl.ds(lax.rem(zz + NZ, NZ) * per + lo, n)]

    def plan(way, h):
        return [way] if h == NZ // 2 else [0, 1]

    def z_copy(way, h, q, arriving=False):
        s = 1 if way == 0 else -1
        from_z = z - s * (h if arriving else h - 1)
        to = dev(x, c, y, z + s)
        chunk = zchunk(a_all.at[c], from_z, 4 * q, 4, 2 * NY)
        out = [remote(chunk, chunk, z_send.at[way, q, h - 1], z_recv.at[way, q, h - 1], to)]
        if q == 0:
            chunk = zchunk(id_all, from_z, 0, NY, NY)
            out.append(remote(chunk, chunk, zi_send.at[way, h - 1], zi_recv.at[way, h - 1], to))
        return out

    def d_copy(way, h, core, q):
        s = 1 if way == 0 else -1
        chunk = zchunk(a_all.at[core], z - s * h, 4 * q, 4, 2 * NY)
        return remote(chunk, chunk, d_send.at[way, q, h], d_recv.at[way, q, h], dev(x, 1 - c, y, z))

    def z_step(h):
        for q in range(2):
            for way in range(2):
                if q not in plan(way, h):
                    continue
                for copy in z_copy(way, h, q, arriving=True):
                    copy.wait_recv()
                if h < NZ // 2 and q in plan(way, h + 1):
                    for copy in z_copy(way, h + 1, q):
                        copy.start()
                d_copy(way, h, c, q).start()

    nearest = (oy + unmatched) % 2

    def forwards(j, dx, cs, r):
        o = nearest if j == 0 else 1 - nearest
        xs = lax.rem(x - dx + NX, NX)
        dy = lax.rem(y - (2 * c + o) + NY, NY)
        slot, sem = w_all.at[o, xs, cs, r], w_recv.at[o, xs, cs, r]
        marks, marks_sem = wi_all.at[o, xs, cs], wi_recv.at[o, xs, cs]

        def send(d):
            to = (dev(x + 1, c, y, z), dev(x - 1, c, y, z), dev(x, c, y + 1, z), dev(x, c, y - 1, z))[d]
            out = [remote(slot, slot, f_send.at[j, dx, cs, r, d], sem, to)]
            if r == 0:
                out.append(remote(marks, marks, fi_send.at[j, dx, cs, d], marks_sem, to))
            return out

        on_x = (0,) if (dx == 1 and cs == 0) else (1,) if (dx == 3 and cs == 1) else ()
        dy_on = 1 if cs == 0 else 3
        todo = []
        if r == 0:
            if dx != 0:
                todo.append((dy == 0, sum([send(d) for d in on_x + (2, 3)], [])))
            todo.append((dy == dy_on, send(2 + cs)))
        else:
            if dx == 0:
                todo.append((dy == dy_on, send(2 + cs)))
                todo.append((dy != 0, send(0) + send(1)))
            elif on_x:
                todo.append((None, sum([send(d) for d in on_x], [])))
        return todo

    def each(todo, act):
        for cond, copies in todo:

            def run(copies=copies):
                for copy in copies:
                    act(copy)

            if cond is None:
                run()
            else:
                pl.when(cond)(run)

    def group(g):
        j, dx = GROUPS[g]
        o = nearest if j == 0 else 1 - nearest
        xs = lax.rem(x - dx + NX, NX)
        for r in range(2):
            for cs in range(2):
                landed(w_all.at[o, xs, cs, r], w_recv.at[o, xs, cs, r])
                if r == 0:
                    landed(wi_all.at[o, xs, cs], wi_recv.at[o, xs, cs])
                each(forwards(j, dx, cs, r), lambda copy: copy.start())

    def groups(which, *gs):
        @pl.when(unmatched == which)
        def _():
            for g in gs:
                group(g)

    def product(o, p):
        marks = table[...]
        for i in range(NX * 2):
            marks = marks + wi_all[o, i // 2, i % 2]
        merged[p] = marks
        copy = pltpu.make_async_copy(merged.at[p], info.at[p], info_sem.at[p])
        copy.start()
        copy.wait()

        def chunk(i, carry):
            lhs, rhs = [], []
            for t in range(CHUNK):
                row = jnp.maximum(info[p, 2, i * CHUNK + t], 0)
                col = info[p, 3, i * CHUNK + t]
                s = jnp.minimum(info[p, row // TILE, row % TILE], NS - 1)
                lhs.append(jnp.concatenate([a_all[k, s] for k in range(2)], axis=0))
                tile = w_all[o, i // 4, (i // 2) % 2, i % 2, t]
                rhs.append(jnp.concatenate([jnp.where(col == b, tile, jnp.zeros_like(tile)) for b in range(OBLK)], axis=1))
            left = jnp.concatenate(lhs, axis=1)
            right = jnp.concatenate(rhs, axis=0)
            acc[o] += jnp.dot(left, right, preferred_element_type=jnp.float32)
            return carry

        lax.fori_loop(0, NX * 4, chunk, 0)

    def out_copies(o, p, act):
        ys = 2 * c + o
        for k in range(2):
            src, dst, sem = stage.at[p, k], out_ref.at[pl.ds(y * SUB * OBLK, SUB * OBLK)], out_recv.at[y]
            here = (ys == y) & (k == c)

            @pl.when(here)
            def _():
                act(pltpu.make_async_copy(src, dst, sem), True)

            @pl.when(jnp.logical_not(here))
            def _():
                act(remote(src, dst, out_send.at[p, k], sem, dev(x, k, ys, z)), False)

    def finish(o, p):
        for k in range(2):
            for b in range(OBLK):
                wide[pl.ds(b, SUB, stride=OBLK), :] = acc[o, pl.ds(k * SUB, SUB), pl.ds(b * TILE, TILE)]
            stage[p, k] = wide[pl.ds(0, SUB * OBLK), :].astype(jnp.bfloat16)
        out_copies(o, p, lambda copy, local: copy.start())

    own_start((0, 1))
    own_beside()
    for copy in a_local:
        copy.wait()
    for k in (1, 3, 2):
        from_y = lax.rem(y - k + NY, NY) + z * NY
        for b in range(2):
            landed(a_all.at[c, 2 * from_y + b], a0_recv.at[k, b])
        landed(id_all.at[from_y], a0_recv.at[k, 2])
    for q in range(2):
        for way in range(2):
            for copy in z_copy(way, 1, q):
                copy.start()
    own_start((2, 3))
    for q in range(2):
        d_copy(0, 0, c, q).start()

    groups(0, 0)
    z_step(1)
    groups(0, 1, 2, 3)
    groups(1, 0)
    for h in (2, 3, 4, 5):
        z_step(h)
    groups(0, 4, 5, 6)
    groups(1, 1, 2, 3)
    z_step(6)
    z_step(7)
    groups(0, 7)
    groups(1, 4, 5, 6)
    z_step(8)
    for q in range(2):
        d_copy(0, 0, 1 - c, q).wait_recv()
        for h in range(1, NZ // 2 + 1):
            for way in range(2):
                if q in plan(way, h):
                    d_copy(way, h, 1 - c, q).wait_recv()

    table[...] = lax.fori_loop(0, NY * NZ, lambda i, total: total + id_all[i], jnp.zeros((8, TILE), jnp.int32))
    first = (nearest + 1 - unmatched) % 2
    product(first, 0)
    finish(first, 0)
    groups(1, 7)
    product(1 - first, 1)
    finish(1 - first, 1)

    for copy in a0:
        copy.wait_send()
    for r in range(2):
        for d in range(4):
            own_tiles(r, d, targets[d]).wait_send()
            if r == 0:
                own_marks(d, targets[d]).wait_send()

    @pl.when(unmatched == 1)
    def _():
        for r in range(2):
            own_tiles(r, 4, beside).wait_send()
        own_marks(4, beside).wait_send()

    for q in range(2):
        d_copy(0, 0, c, q).wait_send()
        for h in range(1, NZ // 2 + 1):
            for way in range(2):
                if q in plan(way, h):
                    for copy in z_copy(way, h, q):
                        copy.wait_send()
                    d_copy(way, h, c, q).wait_send()
    for j, dx in GROUPS:
        for r in range(2):
            for cs in range(2):
                each(forwards(j, dx, cs, r), lambda copy: copy.wait_send())
    for o, p in ((first, 0), (1 - first, 1)):
        out_copies(o, p, lambda copy, local: None if local else copy.wait_send())
    for k in range(NY):
        landed(out_ref.at[pl.ds(k * SUB * OBLK, SUB * OBLK)], out_recv.at[k])


def on_device(amplitudes, amp_blocks, integrals, integral_rows, integral_cols):
    rows, aslot, tile = amplitudes.shape
    dma, half, vmem, smem = pltpu.SemaphoreType.DMA, NZ // 2, pltpu.VMEM, pltpu.SMEM
    out = pl.pallas_call(
        kernel,
        out_shape=jax.ShapeDtypeStruct((rows * OBLK, tile), jnp.bfloat16),
        in_specs=[
            pl.BlockSpec(memory_space=vmem),
            pl.BlockSpec(memory_space=pl.ANY),
            pl.BlockSpec(memory_space=smem),
            pl.BlockSpec(memory_space=smem),
            pl.BlockSpec(memory_space=smem),
        ],
        out_specs=pl.BlockSpec(memory_space=vmem),
        scratch_shapes=[
            vmem((2, NY * SUB, tile), jnp.bfloat16),
            vmem((2, NS, SUB, tile), jnp.bfloat16),
            vmem((NY * NZ, 8, tile), jnp.int32),
            vmem((2, NX, 2, 2, CHUNK, tile, tile), jnp.bfloat16),
            vmem((2, NX, 2, 8, tile), jnp.int32),
            vmem((2, 2 * SUB, OBLK * tile), jnp.float32),
            vmem((2 * rows, tile), jnp.float32),
            vmem((2, 2, SUB * OBLK, tile), jnp.bfloat16),
            vmem((8, tile), jnp.int32),
            vmem((8, tile), jnp.int32),
            vmem((2, 8, tile), jnp.int32),
            smem((2, 8, tile), jnp.int32),
            vmem((8, tile), jnp.int32),
            dma((NY, 3)), dma((NY, 3)),
            dma((2, 2, half)), dma((2, 2, half)), dma((2, half)), dma((2, half)),
            dma((2, 2, half + 1)), dma((2, 2, half + 1)),
            dma((2, 5)), dma((5,)), dma((2, NX, 2, 2)), dma((2, NX, 2)),
            dma((2, NX, 2, 2, 4)), dma((2, NX, 2, 4)),
            dma((2, 2)), dma((NY,)), dma((2,)),
        ],
        compiler_params=pltpu.CompilerParams(
            collective_id=0, has_side_effects=True, vmem_limit_bytes=56 << 20
        ),
    )(amplitudes.reshape(rows * aslot, tile), integrals, amp_blocks, integral_rows, integral_cols)
    return out.reshape(rows, OBLK, tile)


def solution(mesh):
    return jax.shard_map(
        on_device,
        mesh=mesh,
        in_specs=(
            P("occ", "vir", None),
            P("vir"),
            P("vir", "occ", None, None),
            P("vir", "occ"),
            P("vir", "occ"),
        ),
        out_specs=P("occ", "vir", None),
        check_vma=False,
    )
```

```python
import itertools

import jax
import jax.numpy as jnp
from jax import lax
from jax.experimental import pallas as pl
from jax.experimental.pallas import tpu as pltpu
from jax.sharding import PartitionSpec as P

MESH = pl.DeviceIdType.MESH
OBLK = 4
TILE = 128
NX, NY, NZ = 4, 4, 16
SUB = 96
CHUNK = 8
NS = 128
AWAY = (0, 1, 3, 2)
ZP = len(AWAY)
WP = 1


def kernel(
    a_in, w_in, blocks, rows, cols, out_ref,
    a_src, a_all, id_y, id_all, w_all, wi_all, acc, wide, stage, id_own, wi_own, merged, info, table,
    a0_send, a0_recv, z_send, z_recv, zi_send, zi_recv, d_send, d_recv,
    own_send, owni_send, w_recv, wi_recv, f_send, fi_send, out_send, out_recv, info_sem,
):
    occ, vir = lax.axis_index("occ"), lax.axis_index("vir")
    x, c = occ // 2, lax.rem(occ, 2)
    z, y = vir // NY, lax.rem(vir, NY)
    home = y // 2
    unmatched = (c + home) % 2
    oy = lax.rem(y, 2)

    def dev(xx, cc, yy, zz):
        return (lax.rem(xx + NX, NX) * 2 + cc, lax.rem(zz + NZ, NZ) * NY + lax.rem(yy + NY, NY))

    def remote(src, dst, send, recv, device):
        return pltpu.make_async_remote_copy(
            src_ref=src, dst_ref=dst, send_sem=send, recv_sem=recv, device_id=device, device_id_type=MESH
        )

    def landed(ref, sem):
        pltpu.make_async_copy(ref, ref, sem).wait()

    partners = [dev(x, (c + k) % 2, y + j, z) for j in range(NY) for k in range(2) if (j, k) != (0, 0)]
    partners += [dev(x + s, k, y, z) for s in (1, -1) for k in range(2)]
    partners += [dev(x, c, y, z + s) for s in (1, -1)]
    barrier = pltpu.get_barrier_semaphore()
    for p in partners:
        pl.semaphore_signal(barrier, inc=1, device_id=p, device_id_type=MESH)

    wide[...] = a_in[...].astype(jnp.float32)
    for b in range(2):
        a_src[b] = wide[pl.ds(b, NY * SUB, stride=2), :].astype(jnp.bfloat16)
    sub = lax.broadcasted_iota(jnp.int32, (8, TILE), 0)
    lane = lax.broadcasted_iota(jnp.int32, (8, TILE), 1)
    place_of = sub * TILE + lane
    mark = jnp.zeros((8, TILE), jnp.int32)
    for b in range(2):
        mark = jnp.where(place_of == blocks[b], 2 * vir + b, mark)
    id_own[...] = mark
    mark = jnp.zeros((8, TILE), jnp.int32)
    for t in range(2 * CHUNK):
        here = lane == occ * 2 * CHUNK + t
        mark = jnp.where(here & (sub == 2), rows[0, t], mark)
        local = jnp.where(rows[0, t] >= 0, cols[0, t] - vir * OBLK, OBLK)
        mark = jnp.where(here & (sub == 3), local, mark)
    wi_own[...] = mark
    acc[...] = jnp.zeros_like(acc)

    pl.semaphore_wait(barrier, len(partners))

    a_local = []
    for b in range(2):
        a_local.append(pltpu.make_async_copy(a_src.at[b, pl.ds(y * SUB, SUB)], a_all.at[c, 2 * vir + b], a0_recv.at[0, b]))
    a_local.append(pltpu.make_async_copy(id_own, id_y.at[y], a0_recv.at[0, 2]))
    for copy in a_local:
        copy.start()
    a0 = []
    for k in (1, 3, 2):
        to = lax.rem(y + k, NY)
        for b in range(2):
            src = a_src.at[b, pl.ds(to * SUB, SUB)]
            a0.append(remote(src, a_all.at[c, 2 * vir + b], a0_send.at[k, b], a0_recv.at[k, b], dev(x, c, to, z)))
        a0.append(remote(id_own, id_y.at[y], a0_send.at[k, 2], a0_recv.at[k, 2], dev(x, c, to, z)))
    for copy in a0:
        copy.start()

    mine, mine_sem = w_all.at[oy, x, c], w_recv.at[oy, x, c]
    targets = (dev(x + 1, home, y, z), dev(x - 1, home, y, z), dev(x, home, y + 1, z), dev(x, home, y - 1, z))
    beside = dev(x, home, y, z)
    part = CHUNK // WP

    def w_src(r, w):
        return w_in.at[0, pl.ds(r * CHUNK + w * part, part)]

    def own_tiles(r, w, d, to):
        return remote(w_src(r, w), mine.at[r, w], own_send.at[r, w, d], mine_sem.at[r, w], to)

    def own_marks(d, to):
        return remote(wi_own, wi_all.at[oy, x, c], owni_send.at[d], wi_recv.at[oy, x, c], to)

    def own_start(ds, rs):
        for r in rs:
            for w in range(WP):
                for d in ds:
                    if r == 0 and w == 0:
                        own_marks(d, targets[d]).start()
                    own_tiles(r, w, d, targets[d]).start()

    def own_beside():
        @pl.when(unmatched == 0)
        def _():
            for r in range(2):
                for w in range(WP):
                    pltpu.make_async_copy(w_src(r, w), mine.at[r, w], mine_sem.at[r, w]).start()
            pltpu.make_async_copy(wi_own, wi_all.at[oy, x, c], wi_recv.at[oy, x, c]).start()

        @pl.when(unmatched == 1)
        def _():
            for r in range(2):
                for w in range(WP):
                    own_tiles(r, w, 4, beside).start()
            own_marks(4, beside).start()

    def zchunk(ref, zz, lo, n, per):
        return ref.at[pl.ds(lax.rem(zz + NZ, NZ) * per + lo, n)]

    def plan(way, h):
        return range(way * ZP // 2, (way + 1) * ZP // 2) if h == NZ // 2 else range(ZP)

    def z_copy(way, h, q, arriving=False):
        s = 1 if way == 0 else -1
        from_z = z - s * (h if arriving else h - 1)
        to = dev(x, c, y, z + s)
        chunk = zchunk(a_all.at[c], from_z, 2 * lax.rem(y - AWAY[q] + NY, NY), 2, 2 * NY)
        out = [remote(chunk, chunk, z_send.at[way, q, h - 1], z_recv.at[way, q, h - 1], to)]
        if q == ZP - 1:
            chunk = id_all.at[lax.rem(from_z + NZ, NZ)]
            out.append(remote(chunk, chunk, zi_send.at[way, h - 1], zi_recv.at[way, h - 1], to))
        return out

    def d_copy(way, h, core):
        s = 1 if way == 0 else -1
        chunk = zchunk(a_all.at[core], z - s * h, 0, 2 * NY, 2 * NY)
        return remote(chunk, chunk, d_send.at[way, h], d_recv.at[way, h], dev(x, 1 - c, y, z))

    def d_ways(h):
        return range(1 if h in (0, NZ // 2) else 2)

    def z_step(h):
        for q in range(ZP):
            for way in range(2):
                if q not in plan(way, h):
                    continue
                for copy in z_copy(way, h, q, arriving=True):
                    copy.wait_recv()
                if h < NZ // 2 and q in plan(way, h + 1):
                    for copy in z_copy(way, h + 1, q):
                        copy.start()
        for way in d_ways(h):
            d_copy(way, h, c).start()

    nearest = (oy + unmatched) % 2

    def forwards(j, dx, cs, r, w):
        o = nearest if j == 0 else 1 - nearest
        xs = lax.rem(x - dx + NX, NX)
        dy = lax.rem(y - (2 * c + o) + NY, NY)
        slot, sem = w_all.at[o, xs, cs, r, w], w_recv.at[o, xs, cs, r, w]
        marks, marks_sem = wi_all.at[o, xs, cs], wi_recv.at[o, xs, cs]

        def send(d):
            to = (dev(x + 1, c, y, z), dev(x - 1, c, y, z), dev(x, c, y + 1, z), dev(x, c, y - 1, z))[d]
            out = [remote(slot, slot, f_send.at[j, dx, cs, r, w, d], sem, to)]
            if r == 0 and w == 0:
                out.append(remote(marks, marks, fi_send.at[j, dx, cs, d], marks_sem, to))
            return out

        on_x = (0,) if (dx == 1 and cs == 0) else (1,) if (dx == 3 and cs == 1) else ()
        dy_on = 1 if cs == 0 else 3
        todo = []
        if r == 0:
            if dx != 0:
                todo.append((dy == 0, sum([send(d) for d in on_x + (2, 3)], [])))
            todo.append((dy == dy_on, send(2 + cs)))
        else:
            if dx == 0:
                todo.append((dy == dy_on, send(2 + cs)))
                todo.append((dy != 0, send(0) + send(1)))
            elif on_x:
                todo.append((None, sum([send(d) for d in on_x], [])))
        return todo

    def each(todo, act):
        for cond, copies in todo:

            def run(copies=copies):
                for copy in copies:
                    act(copy)

            if cond is None:
                run()
            else:
                pl.when(cond)(run)

    def take(which, *parts):
        @pl.when(unmatched == which)
        def _():
            for w, (j, dx, r), cs in itertools.product(range(WP), parts, range(2)):
                o = nearest if j == 0 else 1 - nearest
                xs = lax.rem(x - dx + NX, NX)
                landed(w_all.at[o, xs, cs, r, w], w_recv.at[o, xs, cs, r, w])
                if r == 0 and w == 0:
                    landed(wi_all.at[o, xs, cs], wi_recv.at[o, xs, cs])
                each(forwards(j, dx, cs, r, w), lambda copy: copy.start())

    def product(o, p):
        marks = table[...]
        for i in range(NX * 2):
            marks = marks + wi_all[o, i // 2, i % 2]
        merged[p] = marks
        copy = pltpu.make_async_copy(merged.at[p], info.at[p], info_sem.at[p])
        copy.start()
        copy.wait()

        def chunk(i, carry):
            lhs, rhs = [], []
            for t in range(CHUNK):
                row = jnp.maximum(info[p, 2, i * CHUNK + t], 0)
                col = info[p, 3, i * CHUNK + t]
                s = jnp.minimum(info[p, row // TILE, row % TILE], NS - 1)
                lhs.append(jnp.concatenate([a_all[k, s] for k in range(2)], axis=0))
                tile = w_all[o, i // 4, (i // 2) % 2, i % 2, t // part, t % part]
                rhs.append(jnp.concatenate([jnp.where(col == b, tile, jnp.zeros_like(tile)) for b in range(OBLK)], axis=1))
            left = jnp.concatenate(lhs, axis=1)
            right = jnp.concatenate(rhs, axis=0)
            acc[o] += jnp.dot(left, right, preferred_element_type=jnp.float32)
            return carry

        lax.fori_loop(0, NX * 4, chunk, 0, unroll=4)

    def out_copies(o, p, act):
        ys = 2 * c + o
        for k in range(2):
            src, dst, sem = stage.at[p, k], out_ref.at[pl.ds(y * SUB * OBLK, SUB * OBLK)], out_recv.at[y]
            here = (ys == y) & (k == c)

            @pl.when(here)
            def _():
                act(pltpu.make_async_copy(src, dst, sem), True)

            @pl.when(jnp.logical_not(here))
            def _():
                act(remote(src, dst, out_send.at[p, k], sem, dev(x, k, ys, z)), False)

    def finish(o, p):
        for k in range(2):
            for b in range(OBLK):
                wide[pl.ds(b, SUB, stride=OBLK), :] = acc[o, pl.ds(k * SUB, SUB), pl.ds(b * TILE, TILE)]
            stage[p, k] = wide[pl.ds(0, SUB * OBLK), :].astype(jnp.bfloat16)
        out_copies(o, p, lambda copy, local: copy.start())

    for copy in a_local:
        copy.wait()
    for way in range(2):
        for copy in z_copy(way, 1, 0):
            copy.start()
    own_start((0, 1), (0, 1))
    own_start((2, 3), (1, 0))
    own_beside()
    for q in range(1, ZP):
        k = AWAY[q]
        from_y = lax.rem(y - k + NY, NY) + z * NY
        for b in range(2):
            landed(a_all.at[c, 2 * from_y + b], a0_recv.at[k, b])
        landed(id_y.at[lax.rem(y - k + NY, NY)], a0_recv.at[k, 2])
        if q == ZP - 1:
            id_all[z] = id_y[0] + id_y[1] + id_y[2] + id_y[3]
        for way in range(2):
            for copy in z_copy(way, 1, q):
                copy.start()
    d_copy(0, 0, c).start()

    z_step(1)
    take(0, (0, 1, 0), (0, 3, 0), (1, 0, 1))
    take(1, (0, 0, 1))
    z_step(2)
    take(0, (0, 1, 1), (0, 3, 1), (1, 0, 0))
    take(1, (0, 0, 0))
    z_step(3)
    take(0, (0, 2, 0))
    take(1, (1, 0, 1))
    z_step(4)
    take(0, (1, 1, 1), (1, 3, 1))
    take(1, (0, 1, 1), (0, 3, 1))
    z_step(5)
    take(0, (1, 1, 0), (1, 3, 0))
    take(1, (0, 1, 0), (0, 3, 0))
    z_step(6)
    take(0, (1, 2, 0))
    take(1, (0, 2, 0), (1, 1, 1), (1, 3, 1))
    z_step(7)
    z_step(8)
    for h in range(NZ // 2 + 1):
        for way in d_ways(h):
            d_copy(way, h, 1 - c).wait_recv()

    table[...] = lax.fori_loop(0, NZ, lambda i, total: total + id_all[i], jnp.zeros((8, TILE), jnp.int32))
    first = (nearest + 1 - unmatched) % 2
    take(0, (1, 2, 1))
    take(1, (0, 2, 1))
    product(first, 0)
    finish(first, 0)
    take(0, (0, 0, 0), (0, 0, 1), (0, 2, 1))
    take(1, (1, 0, 0), (1, 1, 0), (1, 3, 0), (1, 2, 0), (1, 2, 1))
    product(1 - first, 1)
    finish(1 - first, 1)

    for copy in a0:
        copy.wait_send()
    for d in range(4):
        for r, w in itertools.product(range(2), range(WP)):
            own_tiles(r, w, d, targets[d]).wait_send()
        own_marks(d, targets[d]).wait_send()

    @pl.when(unmatched == 1)
    def _():
        for r, w in itertools.product(range(2), range(WP)):
            own_tiles(r, w, 4, beside).wait_send()
        own_marks(4, beside).wait_send()

    for h in range(NZ // 2 + 1):
        for way in d_ways(h):
            d_copy(way, h, c).wait_send()
        for way in range(2):
            for q in plan(way, h) if h > 0 else ():
                for copy in z_copy(way, h, q):
                    copy.wait_send()
    for j, dx, cs, r, w in itertools.product(range(2), range(NX), range(2), range(2), range(WP)):
        each(forwards(j, dx, cs, r, w), lambda copy: copy.wait_send())
    for o, p in ((first, 0), (1 - first, 1)):
        out_copies(o, p, lambda copy, local: None if local else copy.wait_send())
    for k in range(NY):
        landed(out_ref.at[pl.ds(k * SUB * OBLK, SUB * OBLK)], out_recv.at[k])


def on_device(amplitudes, amp_blocks, integrals, integral_rows, integral_cols):
    rows, aslot, tile = amplitudes.shape
    dma, half, vmem, smem = pltpu.SemaphoreType.DMA, NZ // 2, pltpu.VMEM, pltpu.SMEM
    out = pl.pallas_call(
        kernel,
        out_shape=jax.ShapeDtypeStruct((rows * OBLK, tile), jnp.bfloat16),
        in_specs=[
            pl.BlockSpec(memory_space=vmem),
            pl.BlockSpec(memory_space=pl.ANY),
            pl.BlockSpec(memory_space=smem),
            pl.BlockSpec(memory_space=smem),
            pl.BlockSpec(memory_space=smem),
        ],
        out_specs=pl.BlockSpec(memory_space=vmem),
        scratch_shapes=[
            vmem((2, NY * SUB, tile), jnp.bfloat16),
            vmem((2, NS, SUB, tile), jnp.bfloat16),
            vmem((NY, 8, tile), jnp.int32),
            vmem((NZ, 8, tile), jnp.int32),
            vmem((2, NX, 2, 2, WP, CHUNK // WP, tile, tile), jnp.bfloat16),
            vmem((2, NX, 2, 8, tile), jnp.int32),
            vmem((2, 2 * SUB, OBLK * tile), jnp.float32),
            vmem((2 * rows, tile), jnp.float32),
            vmem((2, 2, SUB * OBLK, tile), jnp.bfloat16),
            vmem((8, tile), jnp.int32),
            vmem((8, tile), jnp.int32),
            vmem((2, 8, tile), jnp.int32),
            smem((2, 8, tile), jnp.int32),
            vmem((8, tile), jnp.int32),
            dma((NY, 3)), dma((NY, 3)),
            dma((2, ZP, half)), dma((2, ZP, half)), dma((2, half)), dma((2, half)),
            dma((2, half + 1)), dma((2, half + 1)),
            dma((2, WP, 5)), dma((5,)), dma((2, NX, 2, 2, WP)), dma((2, NX, 2)),
            dma((2, NX, 2, 2, WP, 4)), dma((2, NX, 2, 4)),
            dma((2, 2)), dma((NY,)), dma((2,)),
        ],
        compiler_params=pltpu.CompilerParams(
            collective_id=0, has_side_effects=True, vmem_limit_bytes=56 << 20
        ),
    )(amplitudes.reshape(rows * aslot, tile), integrals, amp_blocks, integral_rows, integral_cols)
    return out.reshape(rows, OBLK, tile)


def solution(mesh):
    return jax.shard_map(
        on_device,
        mesh=mesh,
        in_specs=(
            P("occ", "vir", None),
            P("vir"),
            P("vir", "occ", None, None),
            P("vir", "occ"),
            P("vir", "occ"),
        ),
        out_specs=P("occ", "vir", None),
        check_vma=False,
    )
```

```python
import itertools

import jax
import jax.numpy as jnp
from jax import lax
from jax.experimental import pallas as pl
from jax.experimental.pallas import tpu as pltpu
from jax.sharding import PartitionSpec as P

MESH = pl.DeviceIdType.MESH
OBLK = 4
TILE = 128
NX, NY, NZ = 4, 4, 16
SUB = 96
CHUNK = 8
NS = 128
ZP = 2
WP = 1


def kernel(
    a_in, w_in, blocks, rows, cols, out_ref,
    a_vm, a_src, a_all, id_y, id_all, w_all, wi_all, acc, wide, stage, id_own, wi_own, merged, info, table,
    a0_send, a0_recv, z_send, z_recv, zi_send, zi_recv, d_send, d_recv,
    own_send, owni_send, w_recv, wi_recv, f_send, fi_send, out_send, out_recv, info_sem, in_sem,
):
    occ, vir = lax.axis_index("occ"), lax.axis_index("vir")
    x, c = occ // 2, lax.rem(occ, 2)
    z, y = vir // NY, lax.rem(vir, NY)
    home = y // 2
    unmatched = (c + home) % 2
    oy = lax.rem(y, 2)

    def dev(xx, cc, yy, zz):
        return (lax.rem(xx + NX, NX) * 2 + cc, lax.rem(zz + NZ, NZ) * NY + lax.rem(yy + NY, NY))

    def remote(src, dst, send, recv, device):
        return pltpu.make_async_remote_copy(
            src_ref=src, dst_ref=dst, send_sem=send, recv_sem=recv, device_id=device, device_id_type=MESH
        )

    def landed(ref, sem):
        pltpu.make_async_copy(ref, ref, sem).wait()

    partners = [dev(x, (c + k) % 2, y + j, z) for j in range(NY) for k in range(2) if (j, k) != (0, 0)]
    partners += [dev(x + s, k, y, z) for s in (1, -1) for k in range(2)]
    partners += [dev(x, c, y, z + s) for s in (1, -1)]
    barrier = pltpu.get_barrier_semaphore()
    for p in partners:
        pl.semaphore_signal(barrier, inc=1, device_id=p, device_id_type=MESH)

    fetch = pltpu.make_async_copy(a_in, a_vm, in_sem)
    fetch.start()

    fetch.wait()
    wide[...] = a_vm[...].astype(jnp.float32)
    for b in range(2):
        a_src[b] = wide[pl.ds(b, NY * SUB, stride=2), :].astype(jnp.bfloat16)
    sub = lax.broadcasted_iota(jnp.int32, (8, TILE), 0)
    lane = lax.broadcasted_iota(jnp.int32, (8, TILE), 1)
    place_of = sub * TILE + lane
    mark = jnp.zeros((8, TILE), jnp.int32)
    for b in range(2):
        mark = jnp.where(place_of == blocks[b], 2 * vir + b, mark)
    id_own[...] = mark
    mark = jnp.zeros((8, TILE), jnp.int32)
    for t in range(2 * CHUNK):
        here = lane == occ * 2 * CHUNK + t
        mark = jnp.where(here & (sub == 2), rows[0, t], mark)
        local = jnp.where(rows[0, t] >= 0, cols[0, t] - vir * OBLK, OBLK)
        mark = jnp.where(here & (sub == 3), local, mark)
    wi_own[...] = mark
    acc[...] = jnp.zeros_like(acc)

    pl.semaphore_wait(barrier, len(partners))

    a_local = [
        pltpu.make_async_copy(a_src.at[:, pl.ds(y * SUB, SUB)], a_all.at[c, pl.ds(2 * NY * z, 2)], a0_recv.at[0, 0]),
        pltpu.make_async_copy(id_own, id_y.at[0], a0_recv.at[0, 1]),
    ]
    for copy in a_local:
        copy.start()
    a0 = []
    for k in (1, 3, 2):
        to = lax.rem(y + k, NY)
        src, dst = a_src.at[:, pl.ds(to * SUB, SUB)], a_all.at[c, pl.ds(2 * NY * z + 2 * k, 2)]
        a0.append(remote(src, dst, a0_send.at[k, 0], a0_recv.at[k, 0], dev(x, c, to, z)))
    for k in (1, 3, 2):
        a0.append(remote(id_own, id_y.at[k], a0_send.at[k, 1], a0_recv.at[k, 1], dev(x, c, lax.rem(y + k, NY), z)))
    for copy in a0:
        copy.start()

    mine, mine_sem = w_all.at[oy, x, c], w_recv.at[oy, x, c]
    targets = (dev(x + 1, home, y, z), dev(x - 1, home, y, z), dev(x, home, y + 1, z), dev(x, home, y - 1, z))
    beside = dev(x, home, y, z)
    part = CHUNK // WP

    def w_src(r, w):
        return w_in.at[0, pl.ds(r * CHUNK + w * part, part)]

    def own_tiles(r, w, d, to):
        return remote(w_src(r, w), mine.at[r, w], own_send.at[r, w, d], mine_sem.at[r, w], to)

    def own_marks(d, to):
        return remote(wi_own, wi_all.at[oy, x, c], owni_send.at[d], wi_recv.at[oy, x, c], to)

    def own_start(ds, rs):
        for r in rs:
            for w in range(WP):
                for d in ds:
                    if r == 0 and w == 0:
                        own_marks(d, targets[d]).start()
                    own_tiles(r, w, d, targets[d]).start()

    def own_beside():
        @pl.when(unmatched == 0)
        def _():
            for r in range(2):
                for w in range(WP):
                    pltpu.make_async_copy(w_src(r, w), mine.at[r, w], mine_sem.at[r, w]).start()
            pltpu.make_async_copy(wi_own, wi_all.at[oy, x, c], wi_recv.at[oy, x, c]).start()

        @pl.when(unmatched == 1)
        def _():
            for r in range(2):
                for w in range(WP):
                    own_tiles(r, w, 4, beside).start()
            own_marks(4, beside).start()

    def zchunk(ref, zz, lo, n, per):
        return ref.at[pl.ds(lax.rem(zz + NZ, NZ) * per + lo, n)]

    def plan(way, h):
        return range(way * ZP // 2, (way + 1) * ZP // 2) if h == NZ // 2 else range(ZP)

    def z_copy(way, h, q, arriving=False):
        s = 1 if way == 0 else -1
        from_z = z - s * (h if arriving else h - 1)
        to = dev(x, c, y, z + s)
        chunk = zchunk(a_all.at[c], from_z, q * 2 * NY // ZP, 2 * NY // ZP, 2 * NY)
        out = [remote(chunk, chunk, z_send.at[way, q, h - 1], z_recv.at[way, q, h - 1], to)]
        if q == ZP - 1:
            chunk = id_all.at[lax.rem(from_z + NZ, NZ)]
            out.append(remote(chunk, chunk, zi_send.at[way, h - 1], zi_recv.at[way, h - 1], to))
        return out

    def d_copy(way, h, core):
        s = 1 if way == 0 else -1
        chunk = zchunk(a_all.at[core], z - s * h, 0, 2 * NY, 2 * NY)
        return remote(chunk, chunk, d_send.at[way, h], d_recv.at[way, h], dev(x, 1 - c, y, z))

    def d_ways(h):
        return range(1 if h in (0, NZ // 2) else 2)

    def z_step(h):
        for q in range(ZP):
            for way in range(2):
                if q not in plan(way, h):
                    continue
                for copy in z_copy(way, h, q, arriving=True):
                    copy.wait_recv()
                if h < NZ // 2 and q in plan(way, h + 1):
                    for copy in z_copy(way, h + 1, q):
                        copy.start()
        for way in d_ways(h):
            d_copy(way, h, c).start()

    nearest = (oy + unmatched) % 2

    def forwards(j, dx, cs, r, w):
        o = nearest if j == 0 else 1 - nearest
        xs = lax.rem(x - dx + NX, NX)
        dy = lax.rem(y - (2 * c + o) + NY, NY)
        slot, sem = w_all.at[o, xs, cs, r, w], w_recv.at[o, xs, cs, r, w]
        marks, marks_sem = wi_all.at[o, xs, cs], wi_recv.at[o, xs, cs]

        def send(d):
            to = (dev(x + 1, c, y, z), dev(x - 1, c, y, z), dev(x, c, y + 1, z), dev(x, c, y - 1, z))[d]
            out = [remote(slot, slot, f_send.at[j, dx, cs, r, w, d], sem, to)]
            if r == 0 and w == 0:
                out.append(remote(marks, marks, fi_send.at[j, dx, cs, d], marks_sem, to))
            return out

        on_x = (0,) if (dx == 1 and cs == 0) else (1,) if (dx == 3 and cs == 1) else ()
        dy_on = 1 if cs == 0 else 3
        todo = []
        if r == 0:
            if dx != 0:
                todo.append((dy == 0, sum([send(d) for d in on_x + (2, 3)], [])))
            todo.append((dy == dy_on, send(2 + cs)))
        else:
            if dx == 0:
                todo.append((dy == dy_on, send(2 + cs)))
                todo.append((dy != 0, send(0) + send(1)))
            elif on_x:
                todo.append((None, sum([send(d) for d in on_x], [])))
        return todo

    def each(todo, act):
        for cond, copies in todo:

            def run(copies=copies):
                for copy in copies:
                    act(copy)

            if cond is None:
                run()
            else:
                pl.when(cond)(run)

    def take(which, *parts):
        @pl.when(unmatched == which)
        def _():
            for w, (j, dx, r), cs in itertools.product(range(WP), parts, range(2)):
                o = nearest if j == 0 else 1 - nearest
                xs = lax.rem(x - dx + NX, NX)
                landed(w_all.at[o, xs, cs, r, w], w_recv.at[o, xs, cs, r, w])
                if r == 0 and w == 0:
                    landed(wi_all.at[o, xs, cs], wi_recv.at[o, xs, cs])
                each(forwards(j, dx, cs, r, w), lambda copy: copy.start())

    def product(o, p):
        marks = table[...]
        for i in range(NX * 2):
            marks = marks + wi_all[o, i // 2, i % 2]
        merged[p] = marks
        copy = pltpu.make_async_copy(merged.at[p], info.at[p], info_sem.at[p])
        copy.start()
        copy.wait()

        def chunk(i, carry):
            lhs, rhs = [], []
            for t in range(CHUNK):
                row = jnp.maximum(info[p, 2, i * CHUNK + t], 0)
                col = info[p, 3, i * CHUNK + t]
                s = jnp.minimum(info[p, row // TILE, row % TILE], NS - 1)
                lhs.append(jnp.concatenate([a_all[k, s] for k in range(2)], axis=0))
                tile = w_all[o, i // 4, (i // 2) % 2, i % 2, t // part, t % part]
                rhs.append(jnp.concatenate([jnp.where(col == b, tile, jnp.zeros_like(tile)) for b in range(OBLK)], axis=1))
            left = jnp.concatenate(lhs, axis=1)
            right = jnp.concatenate(rhs, axis=0)
            acc[o] += jnp.dot(left, right, preferred_element_type=jnp.float32)
            return carry

        lax.fori_loop(0, NX * 4, chunk, 0, unroll=8)

    def out_copies(o, p, act):
        ys = 2 * c + o
        for k in range(2):
            src, dst, sem = stage.at[p, k], out_ref.at[pl.ds(y * SUB * OBLK, SUB * OBLK)], out_recv.at[y]
            here = (ys == y) & (k == c)

            @pl.when(here)
            def _():
                act(pltpu.make_async_copy(src, dst, sem), True)

            @pl.when(jnp.logical_not(here))
            def _():
                act(remote(src, dst, out_send.at[p, k], sem, dev(x, k, ys, z)), False)

    def finish(o, p):
        for k in range(2):
            for b in range(OBLK):
                wide[pl.ds(b, SUB, stride=OBLK), :] = acc[o, pl.ds(k * SUB, SUB), pl.ds(b * TILE, TILE)]
            stage[p, k] = wide[pl.ds(0, SUB * OBLK), :].astype(jnp.bfloat16)
        out_copies(o, p, lambda copy, local: copy.start())

    for copy in a_local:
        copy.wait()
    own_start((0, 1), (0, 1))
    own_start((2, 3), (1, 0))
    own_beside()
    for q in range(ZP):
        for k in ((1,), (3, 2))[q]:
            landed(a_all.at[c, pl.ds(2 * NY * z + 2 * k, 2)], a0_recv.at[k, 0])
        if q == ZP - 1:
            for k in (1, 3, 2):
                landed(id_y.at[k], a0_recv.at[k, 1])
            id_all[z] = id_y[0] + id_y[1] + id_y[2] + id_y[3]
        for way in range(2):
            for copy in z_copy(way, 1, q):
                copy.start()
    d_copy(0, 0, c).start()

    z_step(1)
    take(0, (0, 1, 0), (0, 3, 0), (1, 0, 1))
    take(1, (0, 0, 1))
    z_step(2)
    take(0, (0, 1, 1), (0, 3, 1), (1, 0, 0))
    take(1, (0, 0, 0))
    z_step(3)
    z_step(4)
    take(0, (0, 2, 0))
    take(1, (1, 0, 1))
    z_step(5)
    take(0, (1, 1, 1), (1, 3, 1))
    take(1, (0, 1, 1), (0, 3, 1))
    take(0, (1, 1, 0), (1, 3, 0))
    take(1, (0, 1, 0), (0, 3, 0))
    z_step(6)
    z_step(7)
    z_step(8)
    take(0, (1, 2, 0))
    take(1, (0, 2, 0), (1, 1, 1), (1, 3, 1))
    for h in range(NZ // 2 + 1):
        for way in d_ways(h):
            d_copy(way, h, 1 - c).wait_recv()

    slot = lax.fori_loop(0, NZ, lambda i, total: total + id_all[i], jnp.zeros((8, TILE), jnp.int32))
    slot = jnp.minimum(slot, NS - 1)
    come = (y + NY - slot % (2 * NY) // 2) % NY
    table[...] = jnp.where(sub < 2, slot // (2 * NY) * (2 * NY) + 2 * come + slot % 2, 0)
    first = (nearest + 1 - unmatched) % 2
    take(0, (1, 2, 1))
    take(1, (0, 2, 1))
    product(first, 0)
    finish(first, 0)
    take(0, (0, 0, 0), (0, 0, 1), (0, 2, 1))
    take(1, (1, 0, 0), (1, 1, 0), (1, 3, 0), (1, 2, 0), (1, 2, 1))
    product(1 - first, 1)
    finish(1 - first, 1)

    for copy in a0:
        copy.wait_send()
    for d in range(4):
        for r, w in itertools.product(range(2), range(WP)):
            own_tiles(r, w, d, targets[d]).wait_send()
        own_marks(d, targets[d]).wait_send()

    @pl.when(unmatched == 1)
    def _():
        for r, w in itertools.product(range(2), range(WP)):
            own_tiles(r, w, 4, beside).wait_send()
        own_marks(4, beside).wait_send()

    for h in range(NZ // 2 + 1):
        for way in d_ways(h):
            d_copy(way, h, c).wait_send()
        for way in range(2):
            for q in plan(way, h) if h > 0 else ():
                for copy in z_copy(way, h, q):
                    copy.wait_send()
    for j, dx, cs, r, w in itertools.product(range(2), range(NX), range(2), range(2), range(WP)):
        each(forwards(j, dx, cs, r, w), lambda copy: copy.wait_send())
    for o, p in ((first, 0), (1 - first, 1)):
        out_copies(o, p, lambda copy, local: None if local else copy.wait_send())
    for k in range(NY):
        landed(out_ref.at[pl.ds(k * SUB * OBLK, SUB * OBLK)], out_recv.at[k])


def on_device(amplitudes, amp_blocks, integrals, integral_rows, integral_cols):
    rows, aslot, tile = amplitudes.shape
    dma, half, vmem, smem = pltpu.SemaphoreType.DMA, NZ // 2, pltpu.VMEM, pltpu.SMEM
    out = pl.pallas_call(
        kernel,
        out_shape=jax.ShapeDtypeStruct((rows * OBLK, tile), jnp.bfloat16),
        in_specs=[
            pl.BlockSpec(memory_space=pl.ANY),
            pl.BlockSpec(memory_space=pl.ANY),
            pl.BlockSpec(memory_space=smem),
            pl.BlockSpec(memory_space=smem),
            pl.BlockSpec(memory_space=smem),
        ],
        out_specs=pl.BlockSpec(memory_space=pl.ANY),
        scratch_shapes=[
            vmem((2 * rows, tile), jnp.bfloat16),
            vmem((2, NY * SUB, tile), jnp.bfloat16),
            vmem((2, NS, SUB, tile), jnp.bfloat16),
            vmem((NY, 8, tile), jnp.int32),
            vmem((NZ, 8, tile), jnp.int32),
            vmem((2, NX, 2, 2, WP, CHUNK // WP, tile, tile), jnp.bfloat16),
            vmem((2, NX, 2, 8, tile), jnp.int32),
            vmem((2, 2 * SUB, OBLK * tile), jnp.float32),
            vmem((2 * rows, tile), jnp.float32),
            vmem((2, 2, SUB * OBLK, tile), jnp.bfloat16),
            vmem((8, tile), jnp.int32),
            vmem((8, tile), jnp.int32),
            vmem((2, 8, tile), jnp.int32),
            smem((2, 8, tile), jnp.int32),
            vmem((8, tile), jnp.int32),
            dma((NY, 2)), dma((NY, 2)),
            dma((2, ZP, half)), dma((2, ZP, half)), dma((2, half)), dma((2, half)),
            dma((2, half + 1)), dma((2, half + 1)),
            dma((2, WP, 5)), dma((5,)), dma((2, NX, 2, 2, WP)), dma((2, NX, 2)),
            dma((2, NX, 2, 2, WP, 4)), dma((2, NX, 2, 4)),
            dma((2, 2)), dma((NY,)), dma((2,)), dma,
        ],
        compiler_params=pltpu.CompilerParams(
            collective_id=0, has_side_effects=True, vmem_limit_bytes=56 << 20
        ),
    )(amplitudes.reshape(rows * aslot, tile), integrals, amp_blocks, integral_rows, integral_cols)
    return out.reshape(rows, OBLK, tile)


def solution(mesh):
    return jax.shard_map(
        on_device,
        mesh=mesh,
        in_specs=(
            P("occ", "vir", None),
            P("vir"),
            P("vir", "occ", None, None),
            P("vir", "occ"),
            P("vir", "occ"),
        ),
        out_specs=P("occ", "vir", None),
        check_vma=False,
    )
```

```python
import itertools

import jax
import jax.numpy as jnp
from jax import lax
from jax.experimental import pallas as pl
from jax.experimental.pallas import tpu as pltpu
from jax.sharding import PartitionSpec as P

MESH = pl.DeviceIdType.MESH
OBLK = 4
TILE = 128
NX, NY, NZ = 4, 4, 16
SUB = 96
CHUNK = 8
NS = 128
ZP = 2
WP = 1


def kernel(
    a_in, w_in, blocks, rows, cols, out_ref,
    a_vm, a_src, a_all, id_y, id_all, w_all, wi_all, acc, wide, stage, id_own, wi_own, merged, info, table,
    a0_send, a0_recv, z_send, z_recv, zi_send, zi_recv, d_send, d_recv,
    own_send, owni_send, w_recv, wi_recv, f_send, fi_send, out_send, out_recv, info_sem, in_sem,
):
    occ, vir = lax.axis_index("occ"), lax.axis_index("vir")
    x, c = occ // 2, lax.rem(occ, 2)
    z, y = vir // NY, lax.rem(vir, NY)
    home = y // 2
    unmatched = (c + home) % 2
    oy = lax.rem(y, 2)

    def dev(xx, cc, yy, zz):
        return (lax.rem(xx + NX, NX) * 2 + cc, lax.rem(zz + NZ, NZ) * NY + lax.rem(yy + NY, NY))

    def remote(src, dst, send, recv, device):
        return pltpu.make_async_remote_copy(
            src_ref=src, dst_ref=dst, send_sem=send, recv_sem=recv, device_id=device, device_id_type=MESH
        )

    def landed(ref, sem):
        pltpu.make_async_copy(ref, ref, sem).wait()

    partners = [dev(x, (c + k) % 2, y + j, z) for j in range(NY) for k in range(2) if (j, k) != (0, 0)]
    partners += [dev(x + s, k, y, z) for s in (1, -1) for k in range(2)]
    partners += [dev(x, c, y, z + s) for s in (1, -1)]
    barrier = pltpu.get_barrier_semaphore()
    for p in partners:
        pl.semaphore_signal(barrier, inc=1, device_id=p, device_id_type=MESH)

    fetch = pltpu.make_async_copy(a_in, a_vm, in_sem)
    fetch.start()

    fetch.wait()
    wide[...] = a_vm[...].astype(jnp.float32)
    for b in range(2):
        a_src[b] = wide[pl.ds(b, NY * SUB, stride=2), :].astype(jnp.bfloat16)
    sub = lax.broadcasted_iota(jnp.int32, (8, TILE), 0)
    lane = lax.broadcasted_iota(jnp.int32, (8, TILE), 1)
    place_of = sub * TILE + lane
    mark = jnp.zeros((8, TILE), jnp.int32)
    for b in range(2):
        mark = jnp.where(place_of == blocks[b], 2 * vir + b, mark)
    id_own[...] = mark
    mark = jnp.zeros((8, TILE), jnp.int32)
    for t in range(2 * CHUNK):
        here = lane == occ * 2 * CHUNK + t
        mark = jnp.where(here & (sub == 2), rows[0, t], mark)
        local = jnp.where(rows[0, t] >= 0, cols[0, t] - vir * OBLK, OBLK)
        mark = jnp.where(here & (sub == 3), local, mark)
    wi_own[...] = mark
    acc[...] = jnp.zeros_like(acc)

    pl.semaphore_wait(barrier, len(partners))

    a_local = [
        pltpu.make_async_copy(a_src.at[:, pl.ds(y * SUB, SUB)], a_all.at[c, pl.ds(2 * NY * z, 2)], a0_recv.at[0, 0]),
        pltpu.make_async_copy(id_own, id_y.at[0], a0_recv.at[0, 1]),
    ]
    for copy in a_local:
        copy.start()
    a0 = []
    for k in (1, 3, 2):
        to = lax.rem(y + k, NY)
        src, dst = a_src.at[:, pl.ds(to * SUB, SUB)], a_all.at[c, pl.ds(2 * NY * z + 2 * k, 2)]
        a0.append(remote(src, dst, a0_send.at[k, 0], a0_recv.at[k, 0], dev(x, c, to, z)))
    for k in (1, 3, 2):
        a0.append(remote(id_own, id_y.at[k], a0_send.at[k, 1], a0_recv.at[k, 1], dev(x, c, lax.rem(y + k, NY), z)))
    for copy in a0:
        copy.start()

    mine, mine_sem = w_all.at[oy, x, c], w_recv.at[oy, x, c]
    targets = (dev(x + 1, home, y, z), dev(x - 1, home, y, z), dev(x, home, y + 1, z), dev(x, home, y - 1, z))
    beside = dev(x, home, y, z)
    part = CHUNK // WP

    def w_src(r, w):
        return w_in.at[0, pl.ds(r * CHUNK + w * part, part)]

    def own_tiles(r, w, d, to):
        return remote(w_src(r, w), mine.at[r, w], own_send.at[r, w, d], mine_sem.at[r, w], to)

    def own_marks(d, to):
        return remote(wi_own, wi_all.at[oy, x, c], owni_send.at[d], wi_recv.at[oy, x, c], to)

    def own_start(ds, rs):
        for r in rs:
            for w in range(WP):
                for d in ds:
                    if r == 0 and w == 0:
                        own_marks(d, targets[d]).start()
                    own_tiles(r, w, d, targets[d]).start()

    def own_beside():
        @pl.when(unmatched == 0)
        def _():
            for r in range(2):
                for w in range(WP):
                    pltpu.make_async_copy(w_src(r, w), mine.at[r, w], mine_sem.at[r, w]).start()
            pltpu.make_async_copy(wi_own, wi_all.at[oy, x, c], wi_recv.at[oy, x, c]).start()

        @pl.when(unmatched == 1)
        def _():
            for r in range(2):
                for w in range(WP):
                    own_tiles(r, w, 4, beside).start()
            own_marks(4, beside).start()

    def zchunk(ref, zz, lo, n, per):
        return ref.at[pl.ds(lax.rem(zz + NZ, NZ) * per + lo, n)]

    def plan(way, h):
        return range(way * ZP // 2, (way + 1) * ZP // 2) if h == NZ // 2 else range(ZP)

    def z_copy(way, h, q, arriving=False):
        s = 1 if way == 0 else -1
        from_z = z - s * (h if arriving else h - 1)
        to = dev(x, c, y, z + s)
        chunk = zchunk(a_all.at[c], from_z, q * 2 * NY // ZP, 2 * NY // ZP, 2 * NY)
        out = [remote(chunk, chunk, z_send.at[way, q, h - 1], z_recv.at[way, q, h - 1], to)]
        if q == ZP - 1:
            chunk = id_all.at[lax.rem(from_z + NZ, NZ)]
            out.append(remote(chunk, chunk, zi_send.at[way, h - 1], zi_recv.at[way, h - 1], to))
        return out

    def d_copy(way, h, core):
        s = 1 if way == 0 else -1
        chunk = zchunk(a_all.at[core], z - s * h, 0, 2 * NY, 2 * NY)
        return remote(chunk, chunk, d_send.at[way, h], d_recv.at[way, h], dev(x, 1 - c, y, z))

    def d_ways(h):
        return range(1 if h in (0, NZ // 2) else 2)

    def z_step(h):
        for q in range(ZP):
            for way in range(2):
                if q not in plan(way, h):
                    continue
                for copy in z_copy(way, h, q, arriving=True):
                    copy.wait_recv()
                if h < NZ // 2 and q in plan(way, h + 1):
                    for copy in z_copy(way, h + 1, q):
                        copy.start()
        for way in d_ways(h):
            d_copy(way, h, c).start()

    nearest = (oy + unmatched) % 2

    def forwards(j, dx, cs, r, w):
        o = nearest if j == 0 else 1 - nearest
        xs = lax.rem(x - dx + NX, NX)
        dy = lax.rem(y - (2 * c + o) + NY, NY)
        slot, sem = w_all.at[o, xs, cs, r, w], w_recv.at[o, xs, cs, r, w]
        marks, marks_sem = wi_all.at[o, xs, cs], wi_recv.at[o, xs, cs]

        def send(d):
            to = (dev(x + 1, c, y, z), dev(x - 1, c, y, z), dev(x, c, y + 1, z), dev(x, c, y - 1, z))[d]
            out = [remote(slot, slot, f_send.at[j, dx, cs, r, w, d], sem, to)]
            if r == 0 and w == 0:
                out.append(remote(marks, marks, fi_send.at[j, dx, cs, d], marks_sem, to))
            return out

        on_x = (0,) if (dx == 1 and cs == 0) else (1,) if (dx == 3 and cs == 1) else ()
        dy_on = 1 if cs == 0 else 3
        todo = []
        if r == 0:
            if dx != 0:
                todo.append((dy == 0, sum([send(d) for d in on_x + (2, 3)], [])))
            todo.append((dy == dy_on, send(2 + cs)))
        else:
            if dx == 0:
                todo.append((dy == dy_on, send(2 + cs)))
                todo.append((dy != 0, send(0) + send(1)))
            elif on_x:
                todo.append((None, sum([send(d) for d in on_x], [])))
        return todo

    def each(todo, act):
        for cond, copies in todo:

            def run(copies=copies):
                for copy in copies:
                    act(copy)

            if cond is None:
                run()
            else:
                pl.when(cond)(run)

    def take(which, *parts):
        @pl.when(unmatched == which)
        def _():
            for w, (j, dx, r), cs in itertools.product(range(WP), parts, range(2)):
                o = nearest if j == 0 else 1 - nearest
                xs = lax.rem(x - dx + NX, NX)
                landed(w_all.at[o, xs, cs, r, w], w_recv.at[o, xs, cs, r, w])
                if r == 0 and w == 0:
                    landed(wi_all.at[o, xs, cs], wi_recv.at[o, xs, cs])
                each(forwards(j, dx, cs, r, w), lambda copy: copy.start())

    def product(o, p):
        marks = table[...]
        for i in range(NX * 2):
            marks = marks + wi_all[o, i // 2, i % 2]
        merged[p] = marks
        copy = pltpu.make_async_copy(merged.at[p], info.at[p], info_sem.at[p])
        copy.start()
        copy.wait()

        def chunk(i, carry):
            lhs, rhs = [], []
            for t in range(CHUNK):
                row = jnp.maximum(info[p, 2, i * CHUNK + t], 0)
                col = info[p, 3, i * CHUNK + t]
                s = jnp.minimum(info[p, row // TILE, row % TILE], NS - 1)
                lhs.append(jnp.concatenate([a_all[k, s] for k in range(2)], axis=0))
                tile = w_all[o, i // 4, (i // 2) % 2, i % 2, t // part, t % part]
                rhs.append(jnp.concatenate([jnp.where(col == b, tile, jnp.zeros_like(tile)) for b in range(OBLK)], axis=1))
            left = jnp.concatenate(lhs, axis=1)
            right = jnp.concatenate(rhs, axis=0)
            acc[o] += jnp.dot(left, right, preferred_element_type=jnp.float32)
            return carry

        lax.fori_loop(0, NX * 4, chunk, 0, unroll=8)

    def out_copies(o, p, act):
        ys = 2 * c + o
        for k in range(2):
            src, dst, sem = stage.at[p, k], out_ref.at[pl.ds(y * SUB * OBLK, SUB * OBLK)], out_recv.at[y]
            here = (ys == y) & (k == c)

            @pl.when(here)
            def _():
                act(pltpu.make_async_copy(src, dst, sem), True)

            @pl.when(jnp.logical_not(here))
            def _():
                act(remote(src, dst, out_send.at[p, k], sem, dev(x, k, ys, z)), False)

    def finish(o, p):
        for k in range(2):
            for b in range(OBLK):
                wide[pl.ds(b, SUB, stride=OBLK), :] = acc[o, pl.ds(k * SUB, SUB), pl.ds(b * TILE, TILE)]
            stage[p, k] = wide[pl.ds(0, SUB * OBLK), :].astype(jnp.bfloat16)
        out_copies(o, p, lambda copy, local: copy.start())

    for copy in a_local:
        copy.wait()
    own_start((0, 1), (0, 1))
    own_start((2, 3), (1, 0))
    own_beside()
    for q in range(ZP):
        for k in ((1,), (3, 2))[q]:
            landed(a_all.at[c, pl.ds(2 * NY * z + 2 * k, 2)], a0_recv.at[k, 0])
        if q == ZP - 1:
            for k in (1, 3, 2):
                landed(id_y.at[k], a0_recv.at[k, 1])
            id_all[z] = id_y[0] + id_y[1] + id_y[2] + id_y[3]
        for way in range(2):
            for copy in z_copy(way, 1, q):
                copy.start()
    d_copy(0, 0, c).start()

    z_step(1)
    take(0, (0, 1, 0), (0, 3, 0), (1, 0, 1))
    take(1, (0, 0, 1))
    z_step(2)
    take(0, (0, 1, 1), (0, 3, 1), (1, 0, 0))
    take(1, (0, 0, 0))
    z_step(3)
    z_step(4)
    take(0, (0, 2, 0))
    take(1, (1, 0, 1))
    z_step(5)
    take(0, (1, 1, 1), (1, 3, 1))
    take(1, (0, 1, 1), (0, 3, 1))
    take(0, (1, 1, 0), (1, 3, 0))
    take(1, (0, 1, 0), (0, 3, 0))
    z_step(6)
    z_step(7)
    take(0, (1, 2, 0))
    take(1, (0, 2, 0), (1, 1, 1), (1, 3, 1))
    z_step(8)
    for h in range(NZ // 2 + 1):
        for way in d_ways(h):
            d_copy(way, h, 1 - c).wait_recv()

    slot = lax.fori_loop(0, NZ, lambda i, total: total + id_all[i], jnp.zeros((8, TILE), jnp.int32))
    slot = jnp.minimum(slot, NS - 1)
    come = (y + NY - slot % (2 * NY) // 2) % NY
    table[...] = jnp.where(sub < 2, slot // (2 * NY) * (2 * NY) + 2 * come + slot % 2, 0)
    first = (nearest + 1 - unmatched) % 2
    take(0, (1, 2, 1))
    take(1, (0, 2, 1))
    product(first, 0)
    finish(first, 0)
    take(0, (0, 0, 0), (0, 0, 1), (0, 2, 1))
    take(1, (1, 0, 0), (1, 1, 0), (1, 3, 0), (1, 2, 0), (1, 2, 1))
    product(1 - first, 1)
    finish(1 - first, 1)

    for copy in a0:
        copy.wait_send()
    for d in range(4):
        for r, w in itertools.product(range(2), range(WP)):
            own_tiles(r, w, d, targets[d]).wait_send()
        own_marks(d, targets[d]).wait_send()

    @pl.when(unmatched == 1)
    def _():
        for r, w in itertools.product(range(2), range(WP)):
            own_tiles(r, w, 4, beside).wait_send()
        own_marks(4, beside).wait_send()

    for h in range(NZ // 2 + 1):
        for way in d_ways(h):
            d_copy(way, h, c).wait_send()
        for way in range(2):
            for q in plan(way, h) if h > 0 else ():
                for copy in z_copy(way, h, q):
                    copy.wait_send()
    for j, dx, cs, r, w in itertools.product(range(2), range(NX), range(2), range(2), range(WP)):
        each(forwards(j, dx, cs, r, w), lambda copy: copy.wait_send())
    for o, p in ((first, 0), (1 - first, 1)):
        out_copies(o, p, lambda copy, local: None if local else copy.wait_send())
    for k in range(NY):
        landed(out_ref.at[pl.ds(k * SUB * OBLK, SUB * OBLK)], out_recv.at[k])


def on_device(amplitudes, amp_blocks, integrals, integral_rows, integral_cols):
    rows, aslot, tile = amplitudes.shape
    dma, half, vmem, smem = pltpu.SemaphoreType.DMA, NZ // 2, pltpu.VMEM, pltpu.SMEM
    out = pl.pallas_call(
        kernel,
        out_shape=jax.ShapeDtypeStruct((rows * OBLK, tile), jnp.bfloat16),
        in_specs=[
            pl.BlockSpec(memory_space=pl.ANY),
            pl.BlockSpec(memory_space=pl.ANY),
            pl.BlockSpec(memory_space=smem),
            pl.BlockSpec(memory_space=smem),
            pl.BlockSpec(memory_space=smem),
        ],
        out_specs=pl.BlockSpec(memory_space=pl.ANY),
        scratch_shapes=[
            vmem((2 * rows, tile), jnp.bfloat16),
            vmem((2, NY * SUB, tile), jnp.bfloat16),
            vmem((2, NS, SUB, tile), jnp.bfloat16),
            vmem((NY, 8, tile), jnp.int32),
            vmem((NZ, 8, tile), jnp.int32),
            vmem((2, NX, 2, 2, WP, CHUNK // WP, tile, tile), jnp.bfloat16),
            vmem((2, NX, 2, 8, tile), jnp.int32),
            vmem((2, 2 * SUB, OBLK * tile), jnp.float32),
            vmem((2 * rows, tile), jnp.float32),
            vmem((2, 2, SUB * OBLK, tile), jnp.bfloat16),
            vmem((8, tile), jnp.int32),
            vmem((8, tile), jnp.int32),
            vmem((2, 8, tile), jnp.int32),
            smem((2, 8, tile), jnp.int32),
            vmem((8, tile), jnp.int32),
            dma((NY, 2)), dma((NY, 2)),
            dma((2, ZP, half)), dma((2, ZP, half)), dma((2, half)), dma((2, half)),
            dma((2, half + 1)), dma((2, half + 1)),
            dma((2, WP, 5)), dma((5,)), dma((2, NX, 2, 2, WP)), dma((2, NX, 2)),
            dma((2, NX, 2, 2, WP, 4)), dma((2, NX, 2, 4)),
            dma((2, 2)), dma((NY,)), dma((2,)), dma,
        ],
        compiler_params=pltpu.CompilerParams(
            collective_id=0, has_side_effects=True, vmem_limit_bytes=56 << 20
        ),
    )(amplitudes.reshape(rows * aslot, tile), integrals, amp_blocks, integral_rows, integral_cols)
    return out.reshape(rows, OBLK, tile)


def solution(mesh):
    return jax.shard_map(
        on_device,
        mesh=mesh,
        in_specs=(
            P("occ", "vir", None),
            P("vir"),
            P("vir", "occ", None, None),
            P("vir", "occ"),
            P("vir", "occ"),
        ),
        out_specs=P("occ", "vir", None),
        check_vma=False,
    )
```
